256 devices in a mesh: dp: 16 (over x, z_hi), ctx: 16 (over z_lo, y, core).
Axes of the slice: x: 4, y: 4, z: 8 (z_hi: 4, z_lo: 2; z = z_hi * 2 + z_lo), core: 2. Of those that a mesh axis runs over, the one named last changes fastest.
Arguments:
- query: bfloat16 [16, 2048, 4096], P('dp', 'ctx'), may hold values from -6 to 6
- key: bfloat16 [16, 2048, 512], P('dp', 'ctx'), may hold values from -6 to 6
- value: bfloat16 [16, 2048, 512], P('dp', 'ctx'), may hold values from -6 to 6
- d_out: bfloat16 [16, 2048, 4096], P('dp', 'ctx'), may hold values from -6 to 6
- layer_input: bfloat16 [16, 2048, 4096], P('dp', 'ctx'), may hold values from -6 to 6
Outputs:
- attn_out: bfloat16 [16, 2048, 4096], P('dp', 'ctx')
- d_query: bfloat16 [16, 2048, 4096], P('dp', 'ctx')
- d_key: bfloat16 [16, 2048, 512], P('dp', 'ctx')
- d_value: bfloat16 [16, 2048, 512], P('dp', 'ctx')
- d_kv_weight: float32 [4096, 1024], P(('dp', 'ctx'))
The draws below stay inside these ranges and needn't reach their ends.
All inputs are finite; a program needn't handle non-finite values.
Results may differ from the reference program's by a relative error of at most 0.02.
Values may be sent and summed in bfloat16 or wider, within the bound.
No kernel may reach another device: no remote copies, remote signals or barrier semaphores. Data moves between devices by JAX's collectives and lax.ppermute only.
A program may use at most 128 MiB of HBM per device.

```python
import math
import jax
import jax.numpy as jnp
from jax import lax

D = 4096
QH = 32
KVH = 4
HD = 128
SEQS = 16
LENGTH = 2048


def draw_query(key, part):
    key = jax.random.fold_in(key, 11)
    shape = (SEQS, LENGTH, KVH, QH // KVH, HD)
    base = 1.5 * jnp.clip(jax.random.normal(key, shape, jnp.float32), -4.0, 4.0)
    return base.reshape(SEQS, LENGTH, QH * HD).astype(jnp.bfloat16)


def draw_key(key, part):
    key = jax.random.fold_in(key, 23)
    shape = (SEQS, LENGTH, KVH, HD)
    base = jnp.clip(jax.random.normal(key, shape, jnp.float32), -6.0, 6.0)
    return base.reshape(SEQS, LENGTH, KVH * HD).astype(jnp.bfloat16)


def raised(entries, rng, source, target, blocks, factor):
    def block_of(axis_at):
        return (jnp.arange(entries.shape[axis_at]) // (entries.shape[axis_at] // blocks)).reshape((-1,) + (1,) * (entries.ndim - 1 - axis_at))

    one_side = jax.random.permutation(rng, blocks)[block_of(target)]
    second = (block_of(target) + blocks // 2) % blocks
    return jnp.where((block_of(source) == one_side) | (block_of(source) == second), factor * entries, entries)


def steps_of(rng, shape, pieces, smallest, high):
    def one(axis_at, parts):
        draws = jax.random.uniform(jax.random.fold_in(jax.random.fold_in(rng, 6), axis_at), (parts,), jnp.float32, smallest / len(pieces), high / len(pieces))
        return jnp.repeat(jnp.exp(draws), shape[axis_at] // parts).reshape((-1,) + (1,) * (len(shape) - axis_at - 1))

    loudness = one(*pieces[0])
    for cut in pieces[1:]:
        loudness = loudness * one(*cut)
    return loudness


def gaussian(rng, shape, width, bound, split=(), dtype=jnp.bfloat16):
    factor_of = steps_of(rng, shape, split, -0.22, 0.18) if split else 1.0
    values = jax.random.normal(rng, shape, jnp.float32) * width * factor_of
    return jnp.minimum(jnp.maximum(values, -bound), bound).astype(dtype)


def bell_draw_with(stream_key, extent, width, most, split, heavy, held_as=jnp.bfloat16):
    result = width * jax.random.normal(stream_key, extent, jnp.float32)
    if split:
        result = result * steps_of(stream_key, extent, split, -0.22, 0.18)
    return jnp.clip(raised(result, jax.random.fold_in(stream_key, 3), *heavy), -most, most).astype(held_as)


def setup_inputs(seed: int = 0) -> dict:
    key_list = jax.random.split(jax.random.key(seed), 6)
    query = draw_query(jax.random.fold_in(key_list[5], 71), 0)
    key = draw_key(jax.random.fold_in(key_list[5], 71), 0)
    value = gaussian(key_list[2], (SEQS, LENGTH, KVH * HD), 1.0, 6.0, ((0, 16), (1, 16)))
    d_out = gaussian(key_list[3], (SEQS, LENGTH, QH * HD), 1.0, 6.0, ((0, 16), (1, 16)))
    layer_input = bell_draw_with(key_list[4], (SEQS, LENGTH, D), 1.0, 6.0, ((0, 16), (1, 16)), (1, 2, 16, 2.0))
    return dict(query=query, key=key, value=value, d_out=d_out, layer_input=layer_input)


def full_pass(query_head, key_head, value_head, grad_head):
    length = query_head.shape[0]
    inv_root = 1.0 / math.sqrt(HD)
    scores = jnp.dot(query_head, key_head.T, preferred_element_type=jnp.float32) * inv_root
    position = jnp.arange(length)
    scores = jnp.where(position[None, :] <= position[:, None], scores, -1e+30)
    row_max = lax.optimization_barrier(jnp.max(scores, axis=1, keepdims=True))
    weights = jnp.exp(scores - row_max)
    probabilities = weights / lax.optimization_barrier(jnp.sum(weights, axis=1, keepdims=True))
    probs_half = probabilities.astype(jnp.bfloat16)
    out_head = jnp.dot(probs_half, value_head, preferred_element_type=jnp.float32).astype(jnp.bfloat16)
    row_dot = lax.optimization_barrier(jnp.sum(grad_head.astype(jnp.float32) * out_head.astype(jnp.float32), axis=1, keepdims=True))
    d_probs = jnp.dot(grad_head, value_head.T, preferred_element_type=jnp.float32)
    d_scores = (probabilities * (d_probs - row_dot)).astype(jnp.bfloat16)
    query_grad = (jnp.dot(d_scores, key_head, preferred_element_type=jnp.float32) * inv_root).astype(jnp.bfloat16)
    key_grad = jnp.dot(d_scores.T, query_head, preferred_element_type=jnp.float32) * inv_root
    value_grad = jnp.dot(probs_half.T, grad_head, preferred_element_type=jnp.float32)
    return (out_head, query_grad, key_grad, value_grad)

def split_heads(array, heads):
    return array.reshape(SEQS, LENGTH, heads, HD).transpose(0, 2, 1, 3)

def join_heads(array, heads):
    return array.reshape(SEQS, heads, LENGTH, HD).transpose(0, 2, 1, 3).reshape(SEQS, LENGTH, heads * HD)

def reference(query, key, value, d_out, layer_input):
    group = QH // KVH
    query_heads = split_heads(query, QH).reshape(SEQS * QH, LENGTH, HD)
    grad_heads = split_heads(d_out, QH).reshape(SEQS * QH, LENGTH, HD)
    key_heads = jnp.repeat(split_heads(key, KVH), group, axis=1).reshape(SEQS * QH, LENGTH, HD)
    value_heads = jnp.repeat(split_heads(value, KVH), group, axis=1).reshape(SEQS * QH, LENGTH, HD)

    def single(operands):
        return full_pass(operands[0], operands[1], operands[2], operands[3])
    outs, query_grads, key_grads, value_grads = lax.map(single, (query_heads, key_heads, value_heads, grad_heads))
    attn_out = join_heads(outs, QH)
    d_query = join_heads(query_grads, QH)
    key_total = key_grads.reshape(SEQS, KVH, group, LENGTH, HD).sum(axis=2)
    value_total = value_grads.reshape(SEQS, KVH, group, LENGTH, HD).sum(axis=2)
    d_key = join_heads(key_total, KVH).astype(jnp.bfloat16)
    d_value = join_heads(value_total, KVH).astype(jnp.bfloat16)
    joined = jnp.concatenate([d_key, d_value], axis=-1).reshape(SEQS * LENGTH, 2 * KVH * HD)
    d_kv_weight = jnp.dot(layer_input.reshape(SEQS * LENGTH, D).T, joined, preferred_element_type=jnp.float32)
    return (attn_out, d_query, d_key, d_value, d_kv_weight)
```

```python
import functools
import math

import jax
import jax.numpy as jnp
from jax import lax
from jax.experimental import pallas as pl
from jax.experimental.pallas import tpu as pltpu
from jax.sharding import PartitionSpec as P

KVH = 4
HD = 128
HEADS = 8
PAIRS = 4
CHUNK = 256
HALF = 128
INV_ROOT = 1.0 / math.sqrt(HD)
LOG_SCALE = INV_ROOT * math.log2(math.e)
F32 = jnp.float32
BF16 = jnp.bfloat16
NT = (((1,), (1,)), ((), ()))
NN = (((1,), (0,)), ((), ()))


def mul(a, b, dims=NN):
    return lax.dot_general(a, b, dims, preferred_element_type=F32)


def pair(ref, seg, p):
    lo = 2 * p * HD
    return jnp.concatenate(
        [ref[seg, :, lo : lo + HD], ref[seg, :, lo + HD : lo + 2 * HD]], axis=0
    )


def causal(core):
    shape = (CHUNK, 2 * CHUNK)
    key_at = lax.broadcasted_iota(jnp.int32, shape, 0) ^ (core * HALF)
    query_at = (lax.broadcasted_iota(jnp.int32, shape, 1) & (CHUNK - 1)) ^ (core * HALF)
    return key_at <= query_at


def forward_kernel(at, q, kv0, kv1, kv2, kv3, out, lse, keys, values, acc, top, total):
    y, z, core = at[0], at[1], at[2]
    for s, kv in enumerate((kv0, kv1, kv2, kv3)):
        for d in range(2):
            chunk = (z ^ d) * 4 + ((y - s) & 3)
            keys[chunk] = kv[d, :, :HD]
            values[chunk] = kv[d, :, HD:].T
    mask = causal(core)

    for upper in range(2):
        seg = z ^ upper
        top[...] = jnp.full(top.shape, -1e30, F32)
        total[...] = jnp.zeros(total.shape, F32)
        acc[...] = jnp.zeros(acc.shape, F32)

        def visit(chunk, diagonal):
            key, value_t = keys[chunk], values[chunk]
            ahead = mul(key, pair(q, seg, 0), NT)
            for p in range(PAIRS):
                scores = ahead * LOG_SCALE
                if p + 1 < PAIRS:
                    ahead = mul(key, pair(q, seg, p + 1), NT)
                if diagonal:
                    scores = jnp.where(mask, scores, -1e30)
                old = top[p]
                new = jnp.maximum(old, jnp.max(scores, axis=0, keepdims=True))
                weights = jnp.exp2(scores - new)
                shrink = jnp.exp2(old - new)
                top[p] = new
                total[p] = total[p] * shrink + jnp.sum(weights, axis=0, keepdims=True)
                acc[p] = acc[p] * shrink + mul(value_t, weights.astype(BF16))

        def step(chunk, carry):
            visit(chunk, False)
            return carry

        lax.fori_loop(0, upper * 4 + y, step, 0)
        visit(upper * 4 + y, True)
        for p in range(PAIRS):
            lse[seg, p] = top[p] + jnp.log2(total[p])
            rows = (acc[p] * (1.0 / total[p])).T.astype(BF16)
            lo = 2 * p * HD
            out[seg, :, lo : lo + HD] = rows[:CHUNK]
            out[seg, :, lo + HD : lo + 2 * HD] = rows[CHUNK:]


def backward_kernel(shifts, first, last, *refs):
    refs = list(refs)
    at, q, grad, lse = refs[:4]
    del refs[:4]
    kvs = [refs.pop(0) for _ in shifts]
    if first:
        out_in = refs.pop(0)
    else:
        dot_in, dq_in = refs.pop(0), refs.pop(0)
    parts = [refs.pop(0) for _ in shifts]
    if first:
        row_dot = refs.pop(0)
    else:
        row_dot = dot_in
    if last:
        dq_out = refs.pop(0)
        dq, acc = refs
    else:
        dq, acc = refs
    y, z, core = at[0], at[1], at[2]

    if first:
        dq[...] = jnp.zeros(dq.shape, F32)
        for seg in range(2):
            for p in range(PAIRS):
                product = pair(grad, seg, p).astype(F32) * pair(out_in, seg, p).astype(F32)
                row_dot[seg, p] = jnp.sum(product.T, axis=0, keepdims=True)
    else:
        dq[...] = dq_in[...]

    def tile(kv, qseg, kseg, mask, start):
        key, value = kv[kseg, :, :HD], kv[kseg, :, HD:]
        key_t = key.T
        key_sum = value_sum = None

        def front(p):
            query, cot = pair(q, qseg, p), pair(grad, qseg, p)
            return query, cot, mul(key, query, NT), mul(value, cot, NT)

        ahead = front(0)
        for p in range(PAIRS):
            query, cot, scores, d_probs = ahead
            if p + 1 < PAIRS:
                ahead = front(p + 1)
            scores = scores * LOG_SCALE - lse[qseg, p]
            if mask is not None:
                scores = jnp.where(mask, scores, -1e30)
            probs = jnp.exp2(scores)
            d_scores = (probs * (d_probs - row_dot[qseg, p])).astype(BF16)
            value_term = mul(probs.astype(BF16), cot)
            key_term = mul(d_scores, query)
            value_sum = value_term if p == 0 else value_sum + value_term
            key_sum = key_term if p == 0 else key_sum + key_term
            dq[qseg, p] = dq[qseg, p] + mul(key_t, d_scores)
        if start:
            acc[kseg, :, :HD] = key_sum
            acc[kseg, :, HD:] = value_sum
        else:
            acc[kseg, :, :HD] = acc[kseg, :, :HD] + key_sum
            acc[kseg, :, HD:] = acc[kseg, :, HD:] + value_sum

    for s, kv, part in zip(shifts, kvs, parts):
        lower, upper = z, 1 - z
        tile(kv, upper, lower, None, True)
        if s == 0:
            mask = causal(core)
            tile(kv, lower, lower, mask, False)
            tile(kv, upper, upper, mask, True)
        else:
            acc[upper] = jnp.zeros((CHUNK, 2 * HD), F32)

            @pl.when(y >= s)
            def _():
                tile(kv, lower, lower, None, False)
                tile(kv, upper, upper, None, True)

        part[:, :, :HD] = (acc[:, :, :HD] * INV_ROOT).astype(part.dtype)
        part[:, :, HD:] = acc[:, :, HD:].astype(part.dtype)

    if last:
        for seg in range(2):
            for p in range(PAIRS):
                rows = (dq[seg, p] * INV_ROOT).T.astype(BF16)
                lo = 2 * p * HD
                dq_out[seg, :, lo : lo + HD] = rows[:CHUNK]
                dq_out[seg, :, lo + HD : lo + 2 * HD] = rows[CHUNK:]


def project_kernel(x_own, x_other, g0, g1, g2, g3, out):
    total = None
    for s, g in enumerate((g0, g1, g2, g3)):
        for d in range(2):
            left = jnp.concatenate([x_own[d, s], x_other[d, s]], axis=1)
            term = mul(left, g[d])
            total = term if total is None else total + term
    for zl in range(2):
        for y in range(4):
            row = zl * 128 + y * 32
            out[y, 0, zl] = total[row : row + 32].astype(BF16)


VMEM = pl.BlockSpec(memory_space=pltpu.VMEM)
SMEM = pl.BlockSpec(memory_space=pltpu.SMEM)
PARAMS = pltpu.CompilerParams(vmem_limit_bytes=56 << 20)
shape_of = jax.ShapeDtypeStruct
SEG = (2, CHUNK, HEADS * HD)
STAT = (2, PAIRS, 1, 2 * CHUNK)
DQT = (2, PAIRS, HD, 2 * CHUNK)
PART = (2, CHUNK, 2 * HD)


def cost(tiles, products):
    return pl.CostEstimate(
        flops=int(tiles * products * 2 * CHUNK * CHUNK * HD * 3),
        bytes_accessed=4 << 20,
        transcendentals=int(tiles * CHUNK * CHUNK),
    )


def forward(at, q, kvs):
    return pl.pallas_call(
        forward_kernel,
        out_shape=(shape_of(SEG, BF16), shape_of(STAT, F32)),
        in_specs=[SMEM] + [VMEM] * 5,
        out_specs=(VMEM, VMEM),
        scratch_shapes=[
            pltpu.VMEM((8, CHUNK, HD), BF16),
            pltpu.VMEM((8, HD, CHUNK), BF16),
            pltpu.VMEM((PAIRS, HD, 2 * CHUNK), F32),
            pltpu.VMEM((PAIRS, 1, 2 * CHUNK), F32),
            pltpu.VMEM((PAIRS, 1, 2 * CHUNK), F32),
        ],
        compiler_params=PARAMS,
        cost_estimate=cost(96, 2),
        name="forward",
    )(at, q, *kvs)


def backward(shifts, at, q, grad, lse, kvs, more, first, last):
    outs = [shape_of(PART, F32 if s == 0 else BF16) for s in shifts]
    if first:
        outs.append(shape_of(STAT, F32))
    scratch = [pltpu.VMEM(PART, F32)]
    if last:
        outs.append(shape_of(SEG, BF16))
        scratch.insert(0, pltpu.VMEM(DQT, F32))
    else:
        outs.append(shape_of(DQT, F32))
    args = (at, q, grad, lse, *kvs, *more)
    return pl.pallas_call(
        functools.partial(backward_kernel, shifts, first, last),
        out_shape=tuple(outs),
        in_specs=[SMEM] + [VMEM] * (len(args) - 1),
        out_specs=tuple(VMEM for _ in outs),
        scratch_shapes=scratch,
        compiler_params=PARAMS,
        cost_estimate=cost(24 * len(shifts), 5),
        name="backward" + "".join(map(str, shifts)),
    )(*args)


def project(x_own, x_other, gs):
    x_spec = pl.BlockSpec((2, 4, 256, HALF), lambda i: (0, 0, i, 0))
    g_spec = pl.BlockSpec(PART, lambda i: (0, 0, 0))
    return pl.pallas_call(
        project_kernel,
        grid=(4,),
        out_shape=shape_of((4, 4, 2, 32, 2 * HD), BF16),
        in_specs=[x_spec, x_spec] + [g_spec] * 4,
        out_specs=pl.BlockSpec((4, 1, 2, 32, 2 * HD), lambda i: (0, i, 0, 0, 0)),
        compiler_params=PARAMS,
        cost_estimate=pl.CostEstimate(
            flops=2 * 1024 * 2048 * 256, bytes_accessed=6 << 20, transcendentals=0
        ),
        name="project",
    )(x_own, x_other, *gs)


def swap_core(a):
    return lax.ppermute(a, "ctx", [(i, i ^ 1) for i in range(16)])


def swap_z(a):
    return lax.ppermute(a, "ctx", [(i, i ^ 8) for i in range(16)])


def shift_y(a, s):
    return lax.ppermute(
        a, "ctx", [(i, (i & 9) | ((((i >> 1) + s) & 3) << 1)) for i in range(16)]
    )


def shift_x(a, s):
    return lax.ppermute(a, "dp", [(i, (i & 3) | ((((i >> 2) + s) & 3) << 2)) for i in range(16)])


def shift_zh(a, s):
    return lax.ppermute(a, "dp", [(i, (i & 12) | ((i + s) & 3)) for i in range(16)])


def pick(a, index, size, axis):
    return lax.dynamic_slice_in_dim(a, index * size, size, axis)


def local(query, key, value, d_out, layer_input):
    dp, ctx = lax.axis_index("dp"), lax.axis_index("ctx")
    x, zh = dp >> 2, dp & 3
    z, y, core = ctx >> 3, (ctx >> 1) & 3, ctx & 1
    at = jnp.stack([y, z, core]).astype(jnp.int32)

    def gather_heads(a, width):
        mine = pick(a, core, 2 * width, 1)
        other = swap_core(pick(a, 1 - core, 2 * width, 1))
        both = jnp.concatenate([mine, other], axis=0)
        far = swap_z(pick(both, 1 - z, width, 1))
        return jnp.stack([pick(both, z, width, 1), far])

    def return_heads(a, width):
        far = swap_z(a[1])
        both = jnp.stack([jnp.where(z == 0, a[0], far), jnp.where(z == 0, far, a[0])], axis=1)
        mine, other = both[:HALF], swap_core(both[HALF:])
        return jnp.concatenate(
            [jnp.where(core == 0, mine, other), jnp.where(core == 0, other, mine)], axis=1
        )

    pairs = jnp.concatenate(
        [key[0].reshape(HALF, KVH, HD), value[0].reshape(HALF, KVH, HD)], axis=2
    )
    kv = gather_heads(pairs.reshape(HALF, KVH * 2 * HD), 2 * HD)
    kvs = [kv] + [shift_y(kv, s) for s in (1, 2, 3)]
    q = gather_heads(query[0], HEADS * HD)
    grad = gather_heads(d_out[0], HEADS * HD)

    x_t = layer_input[0].T
    pieces = [pick(x_t, x, 1024, 0)]
    pieces += [shift_x(pick(x_t, (x + s) & 3, 1024, 0), s) for s in (1, 2, 3)]
    x_near = jnp.stack(pieces)
    x_own = jnp.stack([x_near, swap_z(x_near)])
    x_other = swap_core(x_own)

    out, lse = forward(at, q, kvs)
    part3, part2, row_dot, dq = backward(
        (3, 2), at, q, grad, lse, (kvs[3], kvs[2]), (out,), True, False
    )
    back3, back2 = shift_y(part3, -3), shift_y(part2, -2)
    part1, dq = backward((1,), at, q, grad, lse, (kvs[1],), (row_dot, dq), False, False)
    back1 = shift_y(part1, -1)
    own, dq = backward((0,), at, q, grad, lse, (kvs[0],), (row_dot, dq), False, True)
    joined = (own + back3.astype(F32) + back2.astype(F32) + back1.astype(F32)).astype(BF16)

    gs = [joined] + [shift_x(joined, s) for s in (1, 2, 3)]
    terms = project(x_own, x_other, gs)
    total = pick(terms, y, 1, 0)[0].astype(F32)
    for s in (1, 2, 3):
        total = total + shift_y(pick(terms, (y + s) & 3, 1, 0)[0], s).astype(F32)
    halves = total.astype(BF16)
    total = pick(halves, zh, 1, 0)[0].astype(F32)
    for s in (1, 2, 3):
        total = total + shift_zh(pick(halves, (zh + s) & 3, 1, 0)[0], s).astype(F32)
    far = swap_z(pick(total, 1 - z, 1, 0)[0])
    near = pick(total, z, 1, 0)[0]
    both = jnp.stack([jnp.where(z == 0, near, far), jnp.where(z == 0, far, near)], axis=1)
    mine = pick(both, core, 16, 0)
    other = swap_core(pick(both, 1 - core, 16, 0))
    rows = jnp.concatenate(
        [jnp.where(core == 0, mine, other), jnp.where(core == 0, other, mine)], axis=1
    )
    weight = jnp.concatenate(
        [rows[:, :, :HD].reshape(16, KVH * HD), rows[:, :, HD:].reshape(16, KVH * HD)], axis=1
    )

    attn_out = return_heads(out, HEADS * HD).reshape(1, HALF, -1)
    d_query = return_heads(dq, HEADS * HD).reshape(1, HALF, -1)
    kv_grad = return_heads(joined, 2 * HD)
    d_key = kv_grad[:, :, :HD].reshape(1, HALF, KVH * HD)
    d_value = kv_grad[:, :, HD:].reshape(1, HALF, KVH * HD)
    return attn_out, d_query, d_key, d_value, weight


def solution(mesh):
    tokens = P("dp", "ctx", None)
    return jax.shard_map(
        local,
        mesh=mesh,
        in_specs=(tokens,) * 5,
        out_specs=(tokens,) * 4 + (P(("dp", "ctx"), None),),
        check_vma=False,
    )
```

```python
import functools
import math

import jax
import jax.numpy as jnp
from jax import lax
from jax.experimental import pallas as pl
from jax.experimental.pallas import tpu as pltpu
from jax.sharding import PartitionSpec as P

KVH = 4
HD = 128
HEADS = 8
PAIRS = 4
WIDE = 1024
CHUNK = 256
HALF = 128
INV_ROOT = 1.0 / math.sqrt(HD)
LOG_SCALE = INV_ROOT * math.log2(math.e)
F32 = jnp.float32
BF16 = jnp.bfloat16
NT = (((1,), (1,)), ((), ()))
NN = (((1,), (0,)), ((), ()))


def mul(a, b, dims=NN):
    return lax.dot_general(a, b, dims, preferred_element_type=F32)


def assemble(at, whole, near, far, rows):
    z, core = at[1], at[2]
    for h in range(HEADS):
        low, mid, high = h * CHUNK, h * CHUNK + HALF, (h + 1) * CHUNK
        here = pl.multiple_of((core * 2 + z) * HEADS * HD + h * HD, HD)
        there = pl.multiple_of(z * HEADS * HD + h * HD, HD)
        rows[0, low:mid] = whole[:, pl.ds(here, HD)]
        rows[0, mid:high] = near[:, pl.ds(there, HD)]
        rows[1, low:high] = far[:, h * HD : (h + 1) * HD]


def write_heads(out, first, rows):
    for i in range(rows.shape[0] // CHUNK):
        lo = (first + i) * HD
        out[:, lo : lo + HD] = rows[i * CHUNK : (i + 1) * CHUNK]


def forward_kernel(
    at, whole, near, far, kv0, kv1, kv2, kv3, here, there, lse, q, out, keys, values, acc, top, total
):
    y, z, core = at[0], at[1], at[2]
    assemble(at, whole, near, far, q)
    for s, kv in enumerate((kv0, kv1, kv2, kv3)):
        for d in range(2):
            chunk = (z ^ d) * 4 + ((y - s) & 3)
            keys[chunk] = kv[d * CHUNK : (d + 1) * CHUNK, :HD]
            values[chunk, :HD] = kv[d * CHUNK : (d + 1) * CHUNK, HD:].T
            values[chunk, HD:] = jnp.ones((16, CHUNK), BF16)

    for upper in range(2):
        seg = z ^ upper
        top[...] = jnp.full(top.shape, -1e30, F32)
        total[...] = jnp.zeros(total.shape, F32)
        acc[...] = jnp.zeros(acc.shape, F32)

        def visit(n, diagonal):
            key = jnp.concatenate([keys[2 * n], keys[2 * n + 1]], axis=0)
            value_t = jnp.concatenate([values[2 * n], values[2 * n + 1]], axis=1)
            ahead = mul(key, q[seg, :WIDE], NT)
            for p in range(2):
                scores = ahead * LOG_SCALE
                if p == 0:
                    ahead = mul(key, q[seg, WIDE:], NT)
                if diagonal:
                    shape = (2 * CHUNK, WIDE)
                    row = lax.broadcasted_iota(jnp.int32, shape, 0)
                    col = lax.broadcasted_iota(jnp.int32, shape, 1) & (CHUNK - 1)
                    key_at = n * (2 * CHUNK) + (row ^ (core * HALF))
                    query_at = (upper * 4 + y) * CHUNK + (col ^ (core * HALF))
                    scores = jnp.where(key_at <= query_at, scores, -1e30)
                old = top[p]
                new = jnp.maximum(old, jnp.max(scores, axis=0, keepdims=True))
                weights = jnp.exp2(scores - new).astype(BF16)
                shrink = jnp.exp2(old - new)
                top[p] = new
                sums = mul(value_t, weights)
                total[p] = total[p] * shrink + sums[HD : HD + 1]
                acc[p] = acc[p] * shrink + sums[:HD]

        def step(n, carry):
            visit(n, False)
            return carry

        full = (upper * 4 + y) >> 1
        lax.fori_loop(0, full, step, 0)
        visit(full, True)
        for p in range(2):
            lse[seg, p] = top[p] + jnp.log2(total[p])
            rows = (acc[p] * (1.0 / total[p])).T.astype(BF16)
            write_heads(out.at[seg], 4 * p, rows)
    here[...], there[...] = out[0], out[1]


def backward_kernel(shifts, first, *refs):
    refs = list(refs)
    at, q, lse = refs[:3]
    del refs[:3]
    kvs = [refs.pop(0) for _ in shifts]
    if first:
        whole, near, far = refs[:3]
        outs = refs[3:5]
        del refs[:5]
    else:
        grad, row_dot, dq_in = refs[:3]
        del refs[:3]
    parts = [refs.pop(0) for _ in shifts]
    if first:
        grad, row_dot, dq, acc = refs
    else:
        dq_outs = refs[:2]
        dq, acc, before, ready = refs[2:]
    y, z, core = at[0], at[1], at[2]

    dq[...] = jnp.zeros(dq.shape, F32)
    if first:
        assemble(at, whole, near, far, grad)
        for seg in range(2):
            for p in range(PAIRS):
                lo = 2 * p * HD
                heads = jnp.concatenate(
                    [outs[seg][:, lo : lo + HD], outs[seg][:, lo + HD : lo + 2 * HD]], axis=0
                )
                cot = grad[seg, p * 2 * CHUNK : (p + 1) * 2 * CHUNK]
                product = cot.astype(F32) * heads.astype(F32)
                row_dot[seg, p] = jnp.sum(product.T, axis=0, keepdims=True)
    else:
        copy = pltpu.make_async_copy(dq_in, before, ready)
        copy.start()

    def tile(kv, qseg, kseg, mask, start):
        rows = pl.ds(pl.multiple_of(kseg * CHUNK, CHUNK), CHUNK)
        key, value = kv[rows, :HD], kv[rows, HD:]
        key_t = key.T
        key_sum = value_sum = None

        def front(p):
            query = q[qseg, p * 2 * CHUNK : (p + 1) * 2 * CHUNK]
            cot = grad[qseg, p * 2 * CHUNK : (p + 1) * 2 * CHUNK]
            return query, cot, mul(key, query, NT), mul(value, cot, NT)

        ahead = front(0)
        for p in range(PAIRS):
            query, cot, scores, d_probs = ahead
            if p + 1 < PAIRS:
                ahead = front(p + 1)
            lo = (p % 2) * 2 * CHUNK
            scores = scores * LOG_SCALE - lse[qseg, p // 2, :, lo : lo + 2 * CHUNK]
            if mask is not None:
                scores = jnp.where(mask, scores, -1e30)
            probs = jnp.exp2(scores)
            d_scores = (probs * (d_probs - row_dot[qseg, p])).astype(BF16)
            value_term = mul(probs.astype(BF16), cot)
            key_term = mul(d_scores, query)
            value_sum = value_term if p == 0 else value_sum + value_term
            key_sum = key_term if p == 0 else key_sum + key_term
            dq[qseg, p] = dq[qseg, p] + mul(key_t, d_scores)
        if start:
            acc[rows, :HD] = key_sum
            acc[rows, HD:] = value_sum
        else:
            acc[rows, :HD] = acc[rows, :HD] + key_sum
            acc[rows, HD:] = acc[rows, HD:] + value_sum

    for s, kv, part in zip(shifts, kvs, parts):
        lower, upper = z, 1 - z
        tile(kv, upper, lower, None, True)
        if s == 0:
            shape = (CHUNK, 2 * CHUNK)
            row = lax.broadcasted_iota(jnp.int32, shape, 0)
            col = lax.broadcasted_iota(jnp.int32, shape, 1) & (CHUNK - 1)
            mask = (row ^ (core * HALF)) <= (col ^ (core * HALF))
            tile(kv, lower, lower, mask, False)
            tile(kv, upper, upper, mask, True)
        else:
            rows = pl.ds(pl.multiple_of(upper * CHUNK, CHUNK), CHUNK)
            acc[rows, :] = jnp.zeros((CHUNK, 2 * HD), F32)

            @pl.when(y >= s)
            def _():
                tile(kv, lower, lower, None, False)
                tile(kv, upper, upper, None, True)

        part[:, :HD] = (acc[:, :HD] * INV_ROOT).astype(part.dtype)
        part[:, HD:] = acc[:, HD:].astype(part.dtype)

    if not first:
        copy.wait()
        for seg in range(2):
            for p in range(PAIRS):
                rows = ((dq[seg, p] + before[seg, p]) * INV_ROOT).T.astype(BF16)
                write_heads(dq_outs[seg], 2 * p, rows)


def project_kernel(at, near, far, near_other, far_other, g0, g1, g2, g3, *refs):
    outs, whole = refs[:4], refs[4]
    left, right = [], []
    for s, g in enumerate((g0, g1, g2, g3)):
        left += [near[s], near_other[s], far[s], far_other[s]]
        right.append(g[...])
    whole[...] = mul(jnp.concatenate(left, axis=1), jnp.concatenate(right, axis=0))
    for i, out in enumerate(outs):
        for zl in range(2):
            row = pl.multiple_of(zl * 128 + ((at[0] + i) & 3) * 32, 32)
            out[0, zl] = whole[pl.ds(row, 32), :].astype(BF16)


def collect_kernel(at, here, far, near, both, out):
    z, core = at[1], at[2]
    width = here.shape[1]
    for dz, dc, rows in ((0, 0, here), (1, 0, far), (0, 1, near), (1, 1, both)):
        lo = pl.multiple_of(((core ^ dc) * 2 + (z ^ dz)) * width, width)
        out[:, pl.ds(lo, width)] = rows[...]


def collect_pairs_kernel(at, here, far, near, both, key, value):
    z, core = at[1], at[2]
    for dz, dc, rows in ((0, 0, here), (1, 0, far), (0, 1, near), (1, 1, both)):
        lo = pl.multiple_of(((core ^ dc) * 2 + (z ^ dz)) * HD, HD)
        key[:, pl.ds(lo, HD)] = rows[:, :HD]
        value[:, pl.ds(lo, HD)] = rows[:, HD:]


def join_kernel(*refs):
    out = refs[-1]
    size = refs[0].shape[0]
    for i, rows in enumerate(refs[:-1]):
        out[i * size : (i + 1) * size] = rows[...]


def turn_kernel(at, rows, token, *outs):
    x = at[3]
    for s in range(4):
        for i in range(8):
            lo = pl.multiple_of(((x + s) & 3) * 1024 + i * HD, HD)
            outs[s][i * HD : (i + 1) * HD] = rows[:, pl.ds(lo, HD)].T


VMEM = pl.BlockSpec(memory_space=pltpu.VMEM)
SMEM = pl.BlockSpec(memory_space=pltpu.SMEM)
HBM = pl.BlockSpec(memory_space=pl.ANY)
PARAMS = pltpu.CompilerParams(vmem_limit_bytes=40 << 20)
shape_of = jax.ShapeDtypeStruct
SIDE = (CHUNK, HEADS * HD)
ROWS = (2, HEADS * CHUNK, HD)
DQT = (2, PAIRS, HD, 2 * CHUNK)
PART = (2 * CHUNK, 2 * HD)


def cost(tiles, products):
    return pl.CostEstimate(
        flops=int(tiles * products * 2 * CHUNK * CHUNK * HD * 3),
        bytes_accessed=4 << 20,
        transcendentals=int(tiles * CHUNK * CHUNK),
    )


def forward(at, whole, near, far, kvs):
    return pl.pallas_call(
        forward_kernel,
        out_shape=(
            shape_of(SIDE, BF16),
            shape_of(SIDE, BF16),
            shape_of((2, 2, 1, WIDE), F32),
            shape_of(ROWS, BF16),
        ),
        in_specs=[SMEM] + [VMEM] * 7,
        out_specs=(VMEM,) * 4,
        scratch_shapes=[
            pltpu.VMEM((2, *SIDE), BF16),
            pltpu.VMEM((8, CHUNK, HD), BF16),
            pltpu.VMEM((8, HD + 16, CHUNK), BF16),
            pltpu.VMEM((2, HD, WIDE), F32),
            pltpu.VMEM((2, 1, WIDE), F32),
            pltpu.VMEM((2, 1, WIDE), F32),
        ],
        compiler_params=PARAMS,
        cost_estimate=cost(96, 2),
        name="forward",
    )(at, whole, near, far, *kvs)


def backward(shifts, first, at, q, lse, kvs, more):
    outs = [shape_of(PART, F32 if s == 0 else BF16) for s in shifts]
    scratch = [pltpu.VMEM(PART, F32)]
    specs = [VMEM] * (2 + len(kvs) + len(more))
    if first:
        outs += [shape_of(ROWS, BF16), shape_of((2, PAIRS, 1, 2 * CHUNK), F32), shape_of(DQT, F32)]
    else:
        outs += [shape_of(SIDE, BF16), shape_of(SIDE, BF16)]
        specs[-1] = HBM
        scratch = [pltpu.VMEM(DQT, F32)] + scratch
        scratch += [pltpu.VMEM(DQT, F32), pltpu.SemaphoreType.DMA]
    return pl.pallas_call(
        functools.partial(backward_kernel, shifts, first),
        out_shape=tuple(outs),
        in_specs=[SMEM] + specs,
        out_specs=(VMEM,) * len(outs),
        scratch_shapes=scratch,
        compiler_params=PARAMS,
        cost_estimate=cost(24 * len(shifts), 5),
        name="backward" + "".join(map(str, shifts)),
    )(at, q, lse, *kvs, *more)


def project(at, xs, gs):
    x_spec = pl.BlockSpec((4, 256, HALF), lambda i: (0, i, 0))
    g_spec = pl.BlockSpec(PART, lambda i: (0, 0))
    return pl.pallas_call(
        project_kernel,
        grid=(4,),
        out_shape=(shape_of((4, 2, 32, 2 * HD), BF16),) * 4,
        in_specs=[SMEM] + [x_spec] * 4 + [g_spec] * 4,
        out_specs=(pl.BlockSpec((1, 2, 32, 2 * HD), lambda i: (i, 0, 0, 0)),) * 4,
        scratch_shapes=[pltpu.VMEM((256, 2 * HD), F32)],
        compiler_params=PARAMS,
        cost_estimate=pl.CostEstimate(
            flops=2 * 1024 * 2048 * 256, bytes_accessed=6 << 20, transcendentals=0
        ),
        name="project",
    )(at, *[rows.reshape(4, 1024, HALF) for rows in xs], *gs)


def split_kernel(at, key, value, own, near, far, both):
    z, core = at[1], at[2]
    for dz, dc, out in ((0, 0, own), (0, 1, near), (1, 0, far), (1, 1, both)):
        lo = pl.multiple_of(((core ^ dc) * 2 + (z ^ dz)) * HD, HD)
        out[:, :HD] = key[:, pl.ds(lo, HD)]
        out[:, HD:] = value[:, pl.ds(lo, HD)]


def split_pairs(at, key, value):
    return pl.pallas_call(
        split_kernel,
        out_shape=(shape_of((HALF, 2 * HD), BF16),) * 4,
        in_specs=[SMEM, VMEM, VMEM],
        out_specs=(VMEM,) * 4,
        compiler_params=PARAMS,
        name="split_pairs",
    )(at, key, value)


def collect(at, here, far, near, both, paired=False):
    width = here.shape[1]
    first = pl.BlockSpec((HALF, width), lambda i: (0, 0))
    second = pl.BlockSpec((HALF, width), lambda i: (1, 0))
    if paired:
        shapes = (shape_of((HALF, KVH * HD), here.dtype),) * 2
        specs = (pl.BlockSpec((HALF, KVH * HD), lambda i: (0, 0)),) * 2
    else:
        shapes = shape_of((HALF, KVH * width), here.dtype)
        specs = pl.BlockSpec((HALF, KVH * width), lambda i: (0, 0))
    return pl.pallas_call(
        collect_pairs_kernel if paired else collect_kernel,
        grid=(1,),
        out_shape=shapes,
        in_specs=[SMEM, first, first, second, second],
        out_specs=specs,
        compiler_params=PARAMS,
        name="collect",
    )(at, here, far, near, both)


def join(*parts):
    rows, width = parts[0].shape
    return pl.pallas_call(
        join_kernel,
        out_shape=shape_of((rows * len(parts), width), parts[0].dtype),
        in_specs=[VMEM] * len(parts),
        out_specs=VMEM,
        compiler_params=PARAMS,
        name="join",
    )(*parts)


def turn(at, rows, token):
    return pl.pallas_call(
        turn_kernel,
        out_shape=(shape_of((1024, HALF), rows.dtype),) * 4,
        in_specs=[SMEM, VMEM, HBM],
        out_specs=(VMEM,) * 4,
        compiler_params=PARAMS,
        name="turn",
    )(at, rows, token)


SWAP = [(0, 1), (1, 0)]


def swap(a, axis):
    return lax.ppermute(a, axis, SWAP)


def swap_both(a):
    return lax.ppermute(a, ("zl", "core"), [(0, 3), (1, 2), (2, 1), (3, 0)])


def shift(a, axis, s):
    return lax.ppermute(a, axis, [(i, (i + s) & 3) for i in range(4)])


def pick(a, index, size, axis):
    return lax.dynamic_slice_in_dim(a, index * size, size, axis)


def tie(*arrays):
    return lax.optimization_barrier(arrays)


def local(query, key, value, d_out, layer_input):
    x, z = lax.axis_index("x"), lax.axis_index("zl")
    y, core = lax.axis_index("y"), lax.axis_index("core")
    at = jnp.stack([y, z, core, x]).astype(jnp.int32)
    query, key, value, d_out = query[0], key[0], value[0], d_out[0]
    layer_input = layer_input[0]

    def group_of(dz, dc):
        return (core ^ dc) * 2 + (z ^ dz)

    def near_heads(a):
        return swap(pick(a, 1 - core, 2 * HEADS * HD, 1), "core")

    def far_heads(a, near):
        return jnp.concatenate(
            [pick(a, group_of(1, 0), HEADS * HD, 1), pick(near, 1 - z, HEADS * HD, 1)], axis=0
        )

    own, near, far, both = split_pairs(at, key, value)
    far, both, near = swap(far, "zl"), swap_both(both), swap(near, "core")
    near, query = tie(near, query)
    q_near = near_heads(query)
    far, both, near, q_send = tie(far, both, near, far_heads(query, q_near))
    kv = join(own, near, far, both)
    kvs = [kv] + [shift(kv, "y", s) for s in (1, 2, 3)]
    q_far = swap(q_send, "zl")
    x_near = turn(at, layer_input, kv)
    x_near = [x_near[0]] + [shift(x_near[s], "x", s) for s in (1, 2, 3)]
    grad_near = near_heads(d_out)
    q_far, grad_send = tie(q_far, far_heads(d_out, grad_near))
    grad_far = swap(grad_send, "zl")

    out, out_there, lse, q = forward(at, query, q_near, q_far, kvs)
    lse, *x_near = tie(lse, *x_near)
    x_near = join(*x_near)
    x_far = swap(x_near, "zl")
    out_far = swap(out_there, "zl")
    part3, part2, part1, grad, row_dot, dq = backward(
        (3, 2, 1), True, at, q, lse, kvs[:0:-1], (d_out, grad_near, grad_far, out, out_there)
    )
    back = [shift(part, "y", s - 4) for s, part in ((1, part3), (2, part2), (3, part1))]
    x_near_other, out_near = swap(x_near, "core"), swap(out, "core")
    row_dot, x_near_other, out_near = tie(row_dot, x_near_other, out_near)
    own, dq, dq_there = backward((0,), False, at, q, lse, kvs[:1], (grad, row_dot, dq))
    joined = own
    for part in back:
        joined = joined + part.astype(F32)
    joined = joined.astype(BF16)
    dq_far = swap(dq_there, "zl")

    joined, x_far, out_far = tie(joined, x_far, out_far)
    gs = [joined] + [shift(joined, "x", s) for s in (1, 2, 3)]
    x_far_other = swap(x_far, "core")
    attn_out = collect(at, out, out_far, out_near, swap(out_far, "core"))
    attn_out, dq_far, joined_far, *gs = tie(attn_out, dq_far, joined[CHUNK:], *gs)
    terms = project(at, (x_near, x_far, x_near_other, x_far_other), gs)

    joined_far = swap(joined_far, "zl")
    moved = [shift(terms[i], "y", i) for i in (1, 2, 3)]
    moved[0], joined_near, joined_far, dq, dq_far = tie(
        moved[0], joined[:CHUNK], joined_far, dq, dq_far
    )
    total = terms[0].astype(F32)
    for term in moved:
        total = total + term.astype(F32)
    d_query = collect(at, dq, dq_far, swap(dq, "core"), swap(dq_far, "core"))
    d_key, d_value = collect(
        at,
        joined_near,
        joined_far,
        swap(joined_near, "core"),
        swap(joined_far, "core"),
        paired=True,
    )

    total, attn_out, d_query, d_key, d_value = tie(
        total.astype(BF16), attn_out, d_query, d_key, d_value
    )
    rows = lax.all_to_all(
        total.reshape(16, 16, 2 * HD), ("zh", "zl", "core"), split_axis=0, concat_axis=0, tiled=True
    )
    rows = rows.reshape(4, 2, 2, 16, 2 * HD).astype(F32).sum(axis=0)
    groups = [rows[zl, c] for c in range(2) for zl in range(2)]
    weight = jnp.concatenate([g[:, :HD] for g in groups] + [g[:, HD:] for g in groups], axis=1)
    return attn_out[None], d_query[None], d_key[None], d_value[None], weight


def solution(mesh):
    parts = jax.sharding.Mesh(mesh.devices.reshape(4, 4, 2, 4, 2), ("x", "zh", "zl", "y", "core"))
    tokens = P(("x", "zh"), ("zl", "y", "core"), None)
    return jax.shard_map(
        local,
        mesh=parts,
        in_specs=(tokens,) * 5,
        out_specs=(tokens,) * 4 + (P(("x", "zh", "zl", "y", "core"), None),),
        check_vma=False,
    )
```

```python
import functools
import math

import jax
import jax.numpy as jnp
from jax import lax
from jax.experimental import pallas as pl
from jax.experimental.pallas import tpu as pltpu
from jax.sharding import PartitionSpec as P

KVH = 4
HD = 128
HEADS = 8
PAIRS = 4
WIDE = 1024
CHUNK = 256
HALF = 128
INV_ROOT = 1.0 / math.sqrt(HD)
LOG_SCALE = INV_ROOT * math.log2(math.e)
F32 = jnp.float32
BF16 = jnp.bfloat16
NT = (((1,), (1,)), ((), ()))
NN = (((1,), (0,)), ((), ()))


def mul(a, b, dims=NN):
    return lax.dot_general(a, b, dims, preferred_element_type=F32)


def assemble(at, whole, near, far, rows):
    z, core = at[1], at[2]
    for h in range(HEADS):
        low, mid, high = h * CHUNK, h * CHUNK + HALF, (h + 1) * CHUNK
        here = pl.multiple_of((core * 2 + z) * HEADS * HD + h * HD, HD)
        there = pl.multiple_of(z * HEADS * HD + h * HD, HD)
        rows[0, low:mid] = whole[:, pl.ds(here, HD)]
        rows[0, mid:high] = near[:, pl.ds(there, HD)]
        rows[1, low:high] = far[:, h * HD : (h + 1) * HD]


def write_heads(out, first, rows):
    for i in range(rows.shape[0] // CHUNK):
        lo = (first + i) * HD
        out[:, lo : lo + HD] = rows[i * CHUNK : (i + 1) * CHUNK]


def forward_kernel(
    at, whole, near, far, kv0, kv1, kv2, kv3, here, there, lse, q, out, keys, values, acc, top, total
):
    y, z, core = at[0], at[1], at[2]
    assemble(at, whole, near, far, q)
    for s, kv in enumerate((kv0, kv1, kv2, kv3)):
        for d in range(2):
            chunk = (z ^ d) * 4 + ((y - s) & 3)
            keys[chunk] = kv[d * CHUNK : (d + 1) * CHUNK, :HD]
            values[chunk, :HD] = kv[d * CHUNK : (d + 1) * CHUNK, HD:].T
            values[chunk, HD:] = jnp.ones((16, CHUNK), BF16)

    for upper in range(2):
        seg = z ^ upper
        top[...] = jnp.full(top.shape, -1e30, F32)
        total[...] = jnp.zeros(total.shape, F32)
        acc[...] = jnp.zeros(acc.shape, F32)

        def visit(n, diagonal):
            key = jnp.concatenate([keys[2 * n], keys[2 * n + 1]], axis=0)
            value_t = jnp.concatenate([values[2 * n], values[2 * n + 1]], axis=1)
            ahead = mul(key, q[seg, :WIDE], NT)
            for p in range(2):
                scores = ahead * LOG_SCALE
                if p == 0:
                    ahead = mul(key, q[seg, WIDE:], NT)
                if diagonal:
                    shape = (2 * CHUNK, WIDE)
                    row = lax.broadcasted_iota(jnp.int32, shape, 0)
                    col = lax.broadcasted_iota(jnp.int32, shape, 1) & (CHUNK - 1)
                    key_at = n * (2 * CHUNK) + (row ^ (core * HALF))
                    query_at = (upper * 4 + y) * CHUNK + (col ^ (core * HALF))
                    scores = jnp.where(key_at <= query_at, scores, -1e30)
                old = top[p]
                new = jnp.maximum(old, jnp.max(scores, axis=0, keepdims=True))
                weights = jnp.exp2(scores - new).astype(BF16)
                shrink = jnp.exp2(old - new)
                top[p] = new
                sums = mul(value_t, weights)
                total[p] = total[p] * shrink + sums[HD : HD + 1]
                acc[p] = acc[p] * shrink + sums[:HD]

        def step(n, carry):
            visit(n, False)
            return carry

        full = (upper * 4 + y) >> 1
        lax.fori_loop(0, full, step, 0)
        visit(full, True)
        for p in range(2):
            lse[seg, p] = top[p] + jnp.log2(total[p])
            rows = (acc[p] * (1.0 / total[p])).T.astype(BF16)
            write_heads(out.at[seg], 4 * p, rows)
    for seg in range(2):
        here[seg * HALF : (seg + 1) * HALF] = out[seg, :HALF]
        there[seg * HALF : (seg + 1) * HALF] = out[seg, HALF:]


def backward_kernel(shifts, first, *refs):
    refs = list(refs)
    at, q, lse = refs[:3]
    del refs[:3]
    kvs = [refs.pop(0) for _ in shifts]
    if first:
        whole, near, far = refs[:3]
        outs = refs[3:5]
        del refs[:5]
    else:
        grad, row_dot, dq_in = refs[:3]
        del refs[:3]
    parts = [refs.pop(0) for _ in shifts]
    if first:
        grad, row_dot, dq, acc = refs
    else:
        dq_outs = refs[:2]
        dq, acc, before, ready = refs[2:]
    y, z, core = at[0], at[1], at[2]

    dq[...] = jnp.zeros(dq.shape, F32)
    if first:
        assemble(at, whole, near, far, grad)
        for seg in range(2):
            for p in range(PAIRS):
                lo = 2 * p * HD
                tokens = slice(seg * HALF, (seg + 1) * HALF)
                heads = jnp.concatenate(
                    [
                        outs[core_side][tokens, at_head : at_head + HD]
                        for at_head in (lo, lo + HD)
                        for core_side in range(2)
                    ],
                    axis=0,
                )
                cot = grad[seg, p * 2 * CHUNK : (p + 1) * 2 * CHUNK]
                product = cot.astype(F32) * heads.astype(F32)
                row_dot[seg, p] = jnp.sum(product.T, axis=0, keepdims=True)
    else:
        copy = pltpu.make_async_copy(dq_in, before, ready)
        copy.start()

    def tile(kv, qseg, kseg, mask, start):
        rows = pl.ds(pl.multiple_of(kseg * CHUNK, CHUNK), CHUNK)
        key, value = kv[rows, :HD], kv[rows, HD:]
        key_t = key.T
        key_sum = value_sum = None

        def front(p):
            query = q[qseg, p * 2 * CHUNK : (p + 1) * 2 * CHUNK]
            cot = grad[qseg, p * 2 * CHUNK : (p + 1) * 2 * CHUNK]
            return query, cot, mul(key, query, NT), mul(value, cot, NT)

        ahead = front(0)
        for p in range(PAIRS):
            query, cot, scores, d_probs = ahead
            if p + 1 < PAIRS:
                ahead = front(p + 1)
            lo = (p % 2) * 2 * CHUNK
            scores = scores * LOG_SCALE - lse[qseg, p // 2, :, lo : lo + 2 * CHUNK]
            if mask is not None:
                scores = jnp.where(mask, scores, -1e30)
            probs = jnp.exp2(scores)
            d_scores = (probs * (d_probs - row_dot[qseg, p])).astype(BF16)
            value_term = mul(probs.astype(BF16), cot)
            key_term = mul(d_scores, query)
            value_sum = value_term if p == 0 else value_sum + value_term
            key_sum = key_term if p == 0 else key_sum + key_term
            dq[qseg, p] = dq[qseg, p] + mul(key_t, d_scores)
        if start:
            acc[rows, :HD] = key_sum
            acc[rows, HD:] = value_sum
        else:
            acc[rows, :HD] = acc[rows, :HD] + key_sum
            acc[rows, HD:] = acc[rows, HD:] + value_sum

    for s, kv, part in zip(shifts, kvs, parts):
        lower, upper = z, 1 - z
        tile(kv, upper, lower, None, True)
        if s == 0:
            shape = (CHUNK, 2 * CHUNK)
            row = lax.broadcasted_iota(jnp.int32, shape, 0)
            col = lax.broadcasted_iota(jnp.int32, shape, 1) & (CHUNK - 1)
            mask = (row ^ (core * HALF)) <= (col ^ (core * HALF))
            tile(kv, lower, lower, mask, False)
            tile(kv, upper, upper, mask, True)
        else:
            rows = pl.ds(pl.multiple_of(upper * CHUNK, CHUNK), CHUNK)
            acc[rows, :] = jnp.zeros((CHUNK, 2 * HD), F32)

            @pl.when(y >= s)
            def _():
                tile(kv, lower, lower, None, False)
                tile(kv, upper, upper, None, True)

        part[:, :HD] = (acc[:, :HD] * INV_ROOT).astype(part.dtype)
        part[:, HD:] = acc[:, HD:].astype(part.dtype)

    if not first:
        copy.wait()
        for seg in range(2):
            for p in range(PAIRS):
                rows = ((dq[seg, p] + before[seg, p]) * INV_ROOT).T.astype(BF16)
                for i in range(2):
                    lo = (2 * p + i) * HD
                    for side in range(2):
                        at_row = i * CHUNK + side * HALF
                        dq_outs[side][seg * HALF : (seg + 1) * HALF, lo : lo + HD] = rows[
                            at_row : at_row + HALF
                        ]


def project_kernel(at, near, far, near_other, far_other, g0, g1, g2, g3, *refs):
    outs, whole = refs[:4], refs[4]
    left, right = [], []
    for s, g in enumerate((g0, g1, g2, g3)):
        left += [near[s], near_other[s], far[s], far_other[s]]
        right.append(g[...])
    whole[...] = mul(jnp.concatenate(left, axis=1), jnp.concatenate(right, axis=0))
    for i, out in enumerate(outs):
        for zl in range(2):
            row = pl.multiple_of(zl * 128 + ((at[0] + i) & 3) * 32, 32)
            out[0, zl] = whole[pl.ds(row, 32), :].astype(BF16)


def finish_kernel(terms, out):
    for c in range(2):
        for zl in range(2):
            total = None
            for zh in range(4):
                term = terms[zh * 4 + zl * 2 + c].astype(F32)
                total = term if total is None else total + term
            lo = (c * 2 + zl) * HD
            out[:, lo : lo + HD] = total[:, :HD]
            out[:, KVH * HD + lo : KVH * HD + lo + HD] = total[:, HD:]


def cut_kernel(at, rows, out, ready):
    width = out.shape[1]
    lo = pl.multiple_of((1 - at[2]) * width, width)
    copy = pltpu.make_async_copy(rows.at[:, pl.ds(lo, width)], out, ready)
    copy.start()
    copy.wait()


def cut_far_kernel(at, rows, near, out, ready):
    width = out.shape[1]
    z, core = at[1], at[2]
    lo = pl.multiple_of((core * 2 + 1 - z) * width, width)
    own = pltpu.make_async_copy(rows.at[:, pl.ds(lo, width)], out.at[:HALF], ready.at[0])
    lo = pl.multiple_of((1 - z) * width, width)
    other = pltpu.make_async_copy(near.at[:, pl.ds(lo, width)], out.at[HALF:], ready.at[1])
    own.start()
    other.start()
    own.wait()
    other.wait()


def collect_kernel(at, here, near, far, both, out):
    z, core = at[1], at[2]
    width = here.shape[1]
    for dz, dc, rows in ((0, 0, here), (1, 0, far), (0, 1, near), (1, 1, both)):
        lo = pl.multiple_of(((core ^ dc) * 2 + (z ^ dz)) * width, width)
        out[:, pl.ds(lo, width)] = rows[...]


def collect_pairs_kernel(at, here, near, far, both, key, value):
    z, core = at[1], at[2]
    for dz, dc, rows in ((0, 0, here), (1, 0, far), (0, 1, near), (1, 1, both)):
        lo = pl.multiple_of(((core ^ dc) * 2 + (z ^ dz)) * HD, HD)
        key[:, pl.ds(lo, HD)] = rows[:, :HD]
        value[:, pl.ds(lo, HD)] = rows[:, HD:]


def join_kernel(*refs):
    out = refs[-1]
    size = refs[0].shape[0]
    for i, rows in enumerate(refs[:-1]):
        out[i * size : (i + 1) * size] = rows[...]


def turn_kernel(at, rows, token, *outs):
    x = at[3]
    for s in range(4):
        for i in range(8):
            lo = pl.multiple_of(((x + s) & 3) * 1024 + i * HD, HD)
            outs[s][i * HD : (i + 1) * HD] = rows[:, pl.ds(lo, HD)].T


VMEM = pl.BlockSpec(memory_space=pltpu.VMEM)
SMEM = pl.BlockSpec(memory_space=pltpu.SMEM)
HBM = pl.BlockSpec(memory_space=pl.ANY)
PARAMS = pltpu.CompilerParams(vmem_limit_bytes=28 << 20)
shape_of = jax.ShapeDtypeStruct
SIDE = (CHUNK, HEADS * HD)
ROWS = (2, HEADS * CHUNK, HD)
DQT = (2, PAIRS, HD, 2 * CHUNK)
PART = (2 * CHUNK, 2 * HD)


def cost(tiles, products):
    return pl.CostEstimate(
        flops=int(tiles * products * 2 * CHUNK * CHUNK * HD * 3),
        bytes_accessed=4 << 20,
        transcendentals=int(tiles * CHUNK * CHUNK),
    )


def forward(at, whole, near, far, kvs):
    return pl.pallas_call(
        forward_kernel,
        out_shape=(
            shape_of(SIDE, BF16),
            shape_of(SIDE, BF16),
            shape_of((2, 2, 1, WIDE), F32),
            shape_of(ROWS, BF16),
        ),
        in_specs=[SMEM] + [VMEM] * 7,
        out_specs=(VMEM,) * 4,
        scratch_shapes=[
            pltpu.VMEM((2, *SIDE), BF16),
            pltpu.VMEM((8, CHUNK, HD), BF16),
            pltpu.VMEM((8, HD + 16, CHUNK), BF16),
            pltpu.VMEM((2, HD, WIDE), F32),
            pltpu.VMEM((2, 1, WIDE), F32),
            pltpu.VMEM((2, 1, WIDE), F32),
        ],
        compiler_params=PARAMS,
        cost_estimate=cost(96, 2),
        name="forward",
    )(at, whole, near, far, *kvs)


def backward(shifts, first, at, q, lse, kvs, more):
    outs = [shape_of(PART, F32 if s == 0 else BF16) for s in shifts]
    scratch = [pltpu.VMEM(PART, F32)]
    specs = [VMEM] * (2 + len(kvs) + len(more))
    if first:
        outs += [shape_of(ROWS, BF16), shape_of((2, PAIRS, 1, 2 * CHUNK), F32), shape_of(DQT, F32)]
    else:
        outs += [shape_of(SIDE, BF16), shape_of(SIDE, BF16)]
        specs[-1] = HBM
        scratch = [pltpu.VMEM(DQT, F32)] + scratch
        scratch += [pltpu.VMEM(DQT, F32), pltpu.SemaphoreType.DMA]
    return pl.pallas_call(
        functools.partial(backward_kernel, shifts, first),
        out_shape=tuple(outs),
        in_specs=[SMEM] + specs,
        out_specs=(VMEM,) * len(outs),
        scratch_shapes=scratch,
        compiler_params=PARAMS,
        cost_estimate=cost(24 * len(shifts), 5),
        name="backward" + "".join(map(str, shifts)),
    )(at, q, lse, *kvs, *more)


def project(at, xs, gs):
    x_spec = pl.BlockSpec((4, 256, HALF), lambda i: (0, i, 0))
    g_spec = pl.BlockSpec(PART, lambda i: (0, 0))
    return pl.pallas_call(
        project_kernel,
        grid=(4,),
        out_shape=(shape_of((4, 2, 32, 2 * HD), BF16),) * 4,
        in_specs=[SMEM] + [x_spec] * 4 + [g_spec] * 4,
        out_specs=(pl.BlockSpec((1, 2, 32, 2 * HD), lambda i: (i, 0, 0, 0)),) * 4,
        scratch_shapes=[pltpu.VMEM((256, 2 * HD), F32)],
        compiler_params=PARAMS,
        cost_estimate=pl.CostEstimate(
            flops=2 * 1024 * 2048 * 256, bytes_accessed=6 << 20, transcendentals=0
        ),
        name="project",
    )(at, *[rows.reshape(4, 1024, HALF) for rows in xs], *gs)


def finish(terms):
    return pl.pallas_call(
        finish_kernel,
        out_shape=shape_of((16, 2 * KVH * HD), F32),
        in_specs=[VMEM],
        out_specs=VMEM,
        compiler_params=PARAMS,
        name="finish",
    )(terms)


def cut(at, rows):
    return pl.pallas_call(
        cut_kernel,
        out_shape=shape_of((HALF, 2 * HEADS * HD), BF16),
        in_specs=[SMEM, HBM],
        out_specs=HBM,
        scratch_shapes=[pltpu.SemaphoreType.DMA],
        compiler_params=PARAMS,
        name="cut",
    )(at, rows)


def cut_far(at, rows, near):
    return pl.pallas_call(
        cut_far_kernel,
        out_shape=shape_of(SIDE, BF16),
        in_specs=[SMEM, HBM, HBM],
        out_specs=HBM,
        scratch_shapes=[pltpu.SemaphoreType.DMA((2,))],
        compiler_params=PARAMS,
        name="cut_far",
    )(at, rows, near)


def split_kernel(at, key, value, own, near, far, both):
    z, core = at[1], at[2]
    for dz, dc, out in ((0, 0, own), (0, 1, near), (1, 0, far), (1, 1, both)):
        lo = pl.multiple_of(((core ^ dc) * 2 + (z ^ dz)) * HD, HD)
        out[:, :HD] = key[:, pl.ds(lo, HD)]
        out[:, HD:] = value[:, pl.ds(lo, HD)]


def split_pairs(at, key, value):
    return pl.pallas_call(
        split_kernel,
        out_shape=(shape_of((HALF, 2 * HD), BF16),) * 4,
        in_specs=[SMEM, VMEM, VMEM],
        out_specs=(VMEM,) * 4,
        compiler_params=PARAMS,
        name="split_pairs",
    )(at, key, value)


def half(width, i):
    return pl.BlockSpec((HALF, width), lambda _: (i, 0))


def send_far(*sides):
    rows, width = HALF * len(sides), sides[0].shape[1]
    return pl.pallas_call(
        join_kernel,
        grid=(1,),
        out_shape=shape_of((rows, width), sides[0].dtype),
        in_specs=[half(width, 1)] * len(sides),
        out_specs=pl.BlockSpec((rows, width), lambda _: (0, 0)),
        compiler_params=PARAMS,
        name="send_far",
    )(*sides)


def collect(at, mine, near, far, first=0, paired=False):
    width = mine.shape[1]
    if paired:
        shapes = (shape_of((HALF, KVH * HD), mine.dtype),) * 2
        specs = (pl.BlockSpec((HALF, KVH * HD), lambda _: (0, 0)),) * 2
    else:
        shapes = shape_of((HALF, KVH * width), mine.dtype)
        specs = pl.BlockSpec((HALF, KVH * width), lambda _: (0, 0))
    return pl.pallas_call(
        collect_pairs_kernel if paired else collect_kernel,
        grid=(1,),
        out_shape=shapes,
        in_specs=[SMEM] + [half(width, i) for i in (0, 0, first, first + 1)],
        out_specs=specs,
        compiler_params=PARAMS,
        name="collect",
    )(at, mine, near, far, far)


def join(*parts):
    rows, width = parts[0].shape
    return pl.pallas_call(
        join_kernel,
        out_shape=shape_of((rows * len(parts), width), parts[0].dtype),
        in_specs=[VMEM] * len(parts),
        out_specs=VMEM,
        compiler_params=PARAMS,
        name="join",
    )(*parts)


def turn(at, rows, token):
    return pl.pallas_call(
        turn_kernel,
        out_shape=(shape_of((1024, HALF), rows.dtype),) * 4,
        in_specs=[SMEM, VMEM, HBM],
        out_specs=(VMEM,) * 4,
        compiler_params=PARAMS,
        name="turn",
    )(at, rows, token)


SWAP = [(0, 1), (1, 0)]


def swap(a, axis):
    return lax.ppermute(a, axis, SWAP)


def swap_both(a):
    return lax.ppermute(a, ("zl", "core"), [(0, 3), (1, 2), (2, 1), (3, 0)])


def shift(a, axis, s):
    return lax.ppermute(a, axis, [(i, (i + s) & 3) for i in range(4)])


def tie(*arrays):
    return lax.optimization_barrier(arrays)


def local(query, key, value, d_out, layer_input):
    x, z = lax.axis_index("x"), lax.axis_index("zl")
    y, core = lax.axis_index("y"), lax.axis_index("core")
    at = jnp.stack([y, z, core, x]).astype(jnp.int32)
    query, key, value, d_out = query[0], key[0], value[0], d_out[0]
    layer_input = layer_input[0]

    own, near, far, both = split_pairs(at, key, value)
    far, both, near = swap(far, "zl"), swap_both(both), swap(near, "core")
    near, query = tie(near, query)
    q_near = swap(cut(at, query), "core")
    far, both, near, q_send = tie(far, both, near, cut_far(at, query, q_near))
    kv = join(own, near, far, both)
    kvs = [kv] + [shift(kv, "y", s) for s in (1, 2, 3)]
    q_far = swap(q_send, "zl")
    x_near = turn(at, layer_input, kv)
    x_near = [x_near[0]] + [shift(x_near[s], "x", s) for s in (1, 2, 3)]
    grad_near = swap(cut(at, d_out), "core")
    q_far, grad_send = tie(q_far, cut_far(at, d_out, grad_near))
    grad_far = swap(grad_send, "zl")

    out, out_other, lse, q = forward(at, query, q_near, q_far, kvs)
    lse, *x_near = tie(lse, *x_near)
    x_near = join(*x_near)
    x_far = swap(x_near, "zl")
    part3, part2, part1, grad, row_dot, dq = backward(
        (3, 2, 1), True, at, q, lse, kvs[:0:-1], (d_out, grad_near, grad_far, out, out_other)
    )
    x_near_other, out_near = swap(x_near, "core"), swap(out_other, "core")
    row_dot, x_near_other, out_near = tie(row_dot, x_near_other, out_near)
    own, dq, dq_other = backward((0,), False, at, q, lse, kvs[:1], (grad, row_dot, dq))
    back = [shift(part, "y", s - 4) for s, part in ((1, part3), (2, part2), (3, part1))]
    joined = own
    for part in back:
        joined = joined + part.astype(F32)
    joined = joined.astype(BF16)
    dq_near = swap(dq_other, "core")
    far = send_far(out, out_near, dq, dq_near)
    joined, x_far, far = tie(joined, x_far, far)
    gs = [joined] + [shift(joined, "x", s) for s in (1, 2, 3)]
    x_far_other = swap(x_far, "core")
    far = swap(far, "zl")
    terms = project(at, (x_near, x_far, x_near_other, x_far_other), gs)

    joined, out, dq, terms0 = tie(joined, out, dq, terms[0])
    total = terms0.astype(F32)
    for i in (1, 2, 3):
        total = total + shift(terms[i], "y", i).astype(F32)
    sides = joined.reshape(2, 2, HALF, 2 * HD)
    mine, other = sides[:, 0].reshape(CHUNK, 2 * HD), sides[:, 1].reshape(CHUNK, 2 * HD)
    near = swap(other, "core")
    sent, far = tie(send_far(mine, near), far)
    d_key, d_value = collect(at, mine, near, swap(sent, "zl"), paired=True)
    attn_out = collect(at, out, out_near, far)
    d_query = collect(at, dq, dq_near, far, first=2)

    total, attn_out, d_query, d_key, d_value = tie(
        total.astype(BF16), attn_out, d_query, d_key, d_value
    )
    terms = lax.all_to_all(
        total.reshape(16, 16, 2 * HD), ("zh", "zl", "core"), split_axis=0, concat_axis=0, tiled=True
    )
    return attn_out[None], d_query[None], d_key[None], d_value[None], finish(terms)


def solution(mesh):
    parts = jax.sharding.Mesh(mesh.devices.reshape(4, 4, 2, 4, 2), ("x", "zh", "zl", "y", "core"))
    tokens = P(("x", "zh"), ("zl", "y", "core"), None)
    return jax.shard_map(
        local,
        mesh=parts,
        in_specs=(tokens,) * 5,
        out_specs=(tokens,) * 4 + (P(("x", "zh", "zl", "y", "core"), None),),
        check_vma=False,
    )
```

```python
import functools
import math

import jax
import jax.numpy as jnp
from jax import lax
from jax.experimental import pallas as pl
from jax.experimental.pallas import tpu as pltpu
from jax.sharding import PartitionSpec as P

KVH = 4
HD = 128
HEADS = 8
PAIRS = 4
WIDE = 1024
CHUNK = 256
HALF = 128
INV_ROOT = 1.0 / math.sqrt(HD)
LOG_SCALE = INV_ROOT * math.log2(math.e)
F32 = jnp.float32
BF16 = jnp.bfloat16
NT = (((1,), (1,)), ((), ()))
NN = (((1,), (0,)), ((), ()))


def mul(a, b, dims=NN):
    return lax.dot_general(a, b, dims, preferred_element_type=F32)


def assemble(at, whole, near, far, rows):
    z, core = at[1], at[2]
    for h in range(HEADS):
        low, mid, high = h * CHUNK, h * CHUNK + HALF, (h + 1) * CHUNK
        here = pl.multiple_of((core * 2 + z) * HEADS * HD + h * HD, HD)
        there = pl.multiple_of(z * HEADS * HD + h * HD, HD)
        rows[0, low:mid] = whole[:, pl.ds(here, HD)]
        rows[0, mid:high] = near[:, pl.ds(there, HD)]
        rows[1, low:high] = far[:, h * HD : (h + 1) * HD]


def write_heads(out, first, rows):
    for i in range(rows.shape[0] // CHUNK):
        lo = (first + i) * HD
        out[:, lo : lo + HD] = rows[i * CHUNK : (i + 1) * CHUNK]


def forward_kernel(
    at, whole, near, far, kv0, kv1, kv2, kv3, here, there, lse, q, out, keys, values, acc, top, total
):
    y, z, core = at[0], at[1], at[2]
    assemble(at, whole, near, far, q)
    for s, kv in enumerate((kv0, kv1, kv2, kv3)):
        for d in range(2):
            chunk = (z ^ d) * 4 + ((y - s) & 3)
            keys[chunk] = kv[d * CHUNK : (d + 1) * CHUNK, :HD]
            values[chunk, :HD] = kv[d * CHUNK : (d + 1) * CHUNK, HD:].T
            values[chunk, HD:] = jnp.ones((16, CHUNK), BF16)

    for upper in range(2):
        seg = z ^ upper
        top[...] = jnp.full(top.shape, -1e30, F32)
        total[...] = jnp.zeros(total.shape, F32)
        acc[...] = jnp.zeros(acc.shape, F32)

        def visit(n, diagonal):
            key = jnp.concatenate([keys[2 * n], keys[2 * n + 1]], axis=0)
            value_t = jnp.concatenate([values[2 * n], values[2 * n + 1]], axis=1)
            ahead = mul(key, q[seg, :WIDE], NT)
            for p in range(2):
                scores = ahead * LOG_SCALE
                if p == 0:
                    ahead = mul(key, q[seg, WIDE:], NT)
                if diagonal:
                    shape = (2 * CHUNK, WIDE)
                    row = lax.broadcasted_iota(jnp.int32, shape, 0)
                    col = lax.broadcasted_iota(jnp.int32, shape, 1) & (CHUNK - 1)
                    key_at = n * (2 * CHUNK) + (row ^ (core * HALF))
                    query_at = (upper * 4 + y) * CHUNK + (col ^ (core * HALF))
                    scores = jnp.where(key_at <= query_at, scores, -1e30)
                old = top[p]
                new = jnp.maximum(old, jnp.max(scores, axis=0, keepdims=True))
                weights = jnp.exp2(scores - new).astype(BF16)
                shrink = jnp.exp2(old - new)
                top[p] = new
                sums = mul(value_t, weights)
                total[p] = total[p] * shrink + sums[HD : HD + 1]
                acc[p] = acc[p] * shrink + sums[:HD]

        def step(n, carry):
            visit(n, False)
            return carry

        full = (upper * 4 + y) >> 1
        lax.fori_loop(0, full, step, 0)
        visit(full, True)
        for p in range(2):
            lse[seg, p] = top[p] + jnp.log2(total[p])
            rows = (acc[p] * (1.0 / total[p])).T.astype(BF16)
            write_heads(out.at[seg], 4 * p, rows)
    for seg in range(2):
        here[seg * HALF : (seg + 1) * HALF] = out[seg, :HALF]
        there[seg * HALF : (seg + 1) * HALF] = out[seg, HALF:]


def backward_kernel(shifts, first, last, *refs):
    refs = list(refs)
    at, q, lse = refs[:3]
    del refs[:3]
    kvs = [refs.pop(0) for _ in shifts]
    if first:
        whole, near, far = refs[:3]
        outs = refs[3:5]
        del refs[:5]
    else:
        grad, row_dot, dq_in = refs[:3]
        del refs[:3]
    parts = [refs.pop(0) for _ in shifts]
    if first:
        grad, row_dot, dq, acc = refs
    elif not last:
        dq, acc = refs
    else:
        dq_outs = refs[:2]
        dq, acc, before, ready = refs[2:]
    y, z, core = at[0], at[1], at[2]

    if first or last:
        dq[...] = jnp.zeros(dq.shape, F32)
    else:
        dq[...] = dq_in[...]
    if first:
        assemble(at, whole, near, far, grad)
        for seg in range(2):
            for p in range(PAIRS):
                lo = 2 * p * HD
                tokens = slice(seg * HALF, (seg + 1) * HALF)
                heads = jnp.concatenate(
                    [
                        outs[core_side][tokens, at_head : at_head + HD]
                        for at_head in (lo, lo + HD)
                        for core_side in range(2)
                    ],
                    axis=0,
                )
                cot = grad[seg, p * 2 * CHUNK : (p + 1) * 2 * CHUNK]
                product = cot.astype(F32) * heads.astype(F32)
                row_dot[seg, p] = jnp.sum(product.T, axis=0, keepdims=True)
    if last:
        copy = pltpu.make_async_copy(dq_in, before, ready)
        copy.start()

    def tile(kv, qseg, kseg, mask, start):
        rows = pl.ds(pl.multiple_of(kseg * CHUNK, CHUNK), CHUNK)
        key, value = kv[rows, :HD], kv[rows, HD:]
        key_t = key.T
        key_sum = value_sum = None

        def front(p):
            query = q[qseg, p * 2 * CHUNK : (p + 1) * 2 * CHUNK]
            cot = grad[qseg, p * 2 * CHUNK : (p + 1) * 2 * CHUNK]
            return query, cot, mul(key, query, NT), mul(value, cot, NT)

        ahead = front(0)
        for p in range(PAIRS):
            query, cot, scores, d_probs = ahead
            if p + 1 < PAIRS:
                ahead = front(p + 1)
            lo = (p % 2) * 2 * CHUNK
            scores = scores * LOG_SCALE - lse[qseg, p // 2, :, lo : lo + 2 * CHUNK]
            if mask is not None:
                scores = jnp.where(mask, scores, -1e30)
            probs = jnp.exp2(scores)
            d_scores = (probs * (d_probs - row_dot[qseg, p])).astype(BF16)
            value_term = mul(probs.astype(BF16), cot)
            key_term = mul(d_scores, query)
            value_sum = value_term if p == 0 else value_sum + value_term
            key_sum = key_term if p == 0 else key_sum + key_term
            dq[qseg, p] = dq[qseg, p] + mul(key_t, d_scores)
        if start:
            acc[rows, :HD] = key_sum
            acc[rows, HD:] = value_sum
        else:
            acc[rows, :HD] = acc[rows, :HD] + key_sum
            acc[rows, HD:] = acc[rows, HD:] + value_sum

    for s, kv, part in zip(shifts, kvs, parts):
        lower, upper = z, 1 - z
        tile(kv, upper, lower, None, True)
        if s == 0:
            shape = (CHUNK, 2 * CHUNK)
            row = lax.broadcasted_iota(jnp.int32, shape, 0)
            col = lax.broadcasted_iota(jnp.int32, shape, 1) & (CHUNK - 1)
            mask = (row ^ (core * HALF)) <= (col ^ (core * HALF))
            tile(kv, lower, lower, mask, False)
            tile(kv, upper, upper, mask, True)
        else:
            rows = pl.ds(pl.multiple_of(upper * CHUNK, CHUNK), CHUNK)
            acc[rows, :] = jnp.zeros((CHUNK, 2 * HD), F32)

            @pl.when(y >= s)
            def _():
                tile(kv, lower, lower, None, False)
                tile(kv, upper, upper, None, True)

        part[:, :HD] = (acc[:, :HD] * INV_ROOT).astype(part.dtype)
        part[:, HD:] = acc[:, HD:].astype(part.dtype)

    if last:
        copy.wait()
        for seg in range(2):
            for p in range(PAIRS):
                rows = ((dq[seg, p] + before[seg, p]) * INV_ROOT).T.astype(BF16)
                for i in range(2):
                    lo = (2 * p + i) * HD
                    for side in range(2):
                        at_row = i * CHUNK + side * HALF
                        dq_outs[side][seg * HALF : (seg + 1) * HALF, lo : lo + HD] = rows[
                            at_row : at_row + HALF
                        ]


def project_kernel(at, near, far, near_other, far_other, g0, g1, g2, g3, *refs):
    outs, whole = refs[:4], refs[4]
    left, right = [], []
    for s, g in enumerate((g0, g1, g2, g3)):
        left += [near[s], near_other[s], far[s], far_other[s]]
        right.append(g[...])
    whole[...] = mul(jnp.concatenate(left, axis=1), jnp.concatenate(right, axis=0))
    for i, out in enumerate(outs):
        for zl in range(2):
            row = pl.multiple_of(zl * 128 + ((at[0] + i) & 3) * 32, 32)
            out[0, zl] = whole[pl.ds(row, 32), :].astype(BF16)


def finish_kernel(terms, out):
    for c in range(2):
        for zl in range(2):
            total = None
            for zh in range(4):
                term = terms[zh * 4 + zl * 2 + c].astype(F32)
                total = term if total is None else total + term
            lo = (c * 2 + zl) * HD
            out[:, lo : lo + HD] = total[:, :HD]
            out[:, KVH * HD + lo : KVH * HD + lo + HD] = total[:, HD:]


def cut_kernel(at, rows, out, ready):
    width = out.shape[1]
    lo = pl.multiple_of((1 - at[2]) * width, width)
    copy = pltpu.make_async_copy(rows.at[:, pl.ds(lo, width)], out, ready)
    copy.start()
    copy.wait()


def cut_far_kernel(at, rows, near, out, ready):
    width = out.shape[1]
    z, core = at[1], at[2]
    lo = pl.multiple_of((core * 2 + 1 - z) * width, width)
    own = pltpu.make_async_copy(rows.at[:, pl.ds(lo, width)], out.at[:HALF], ready.at[0])
    lo = pl.multiple_of((1 - z) * width, width)
    other = pltpu.make_async_copy(near.at[:, pl.ds(lo, width)], out.at[HALF:], ready.at[1])
    own.start()
    other.start()
    own.wait()
    other.wait()


def collect_kernel(at, here, near, far, both, out):
    z, core = at[1], at[2]
    width = here.shape[1]
    for dz, dc, rows in ((0, 0, here), (1, 0, far), (0, 1, near), (1, 1, both)):
        lo = pl.multiple_of(((core ^ dc) * 2 + (z ^ dz)) * width, width)
        out[:, pl.ds(lo, width)] = rows[...]


def collect_pairs_kernel(at, here, near, far, both, key, value):
    z, core = at[1], at[2]
    for dz, dc, rows in ((0, 0, here), (1, 0, far), (0, 1, near), (1, 1, both)):
        lo = pl.multiple_of(((core ^ dc) * 2 + (z ^ dz)) * HD, HD)
        key[:, pl.ds(lo, HD)] = rows[:, :HD]
        value[:, pl.ds(lo, HD)] = rows[:, HD:]


def join_kernel(*refs):
    out = refs[-1]
    size = refs[0].shape[0]
    for i, rows in enumerate(refs[:-1]):
        out[i * size : (i + 1) * size] = rows[...]


def turn_kernel(at, rows, token, *outs):
    x = at[3]
    for s in range(4):
        for i in range(8):
            lo = pl.multiple_of(((x + s) & 3) * 1024 + i * HD, HD)
            outs[s][i * HD : (i + 1) * HD] = rows[:, pl.ds(lo, HD)].T


VMEM = pl.BlockSpec(memory_space=pltpu.VMEM)
SMEM = pl.BlockSpec(memory_space=pltpu.SMEM)
HBM = pl.BlockSpec(memory_space=pl.ANY)
PARAMS = pltpu.CompilerParams(vmem_limit_bytes=28 << 20)
shape_of = jax.ShapeDtypeStruct
SIDE = (CHUNK, HEADS * HD)
ROWS = (2, HEADS * CHUNK, HD)
DQT = (2, PAIRS, HD, 2 * CHUNK)
PART = (2 * CHUNK, 2 * HD)


def cost(tiles, products):
    return pl.CostEstimate(
        flops=int(tiles * products * 2 * CHUNK * CHUNK * HD * 3),
        bytes_accessed=4 << 20,
        transcendentals=int(tiles * CHUNK * CHUNK),
    )


def forward(at, whole, near, far, kvs):
    return pl.pallas_call(
        forward_kernel,
        out_shape=(
            shape_of(SIDE, BF16),
            shape_of(SIDE, BF16),
            shape_of((2, 2, 1, WIDE), F32),
            shape_of(ROWS, BF16),
        ),
        in_specs=[SMEM] + [VMEM] * 7,
        out_specs=(VMEM,) * 4,
        scratch_shapes=[
            pltpu.VMEM((2, *SIDE), BF16),
            pltpu.VMEM((8, CHUNK, HD), BF16),
            pltpu.VMEM((8, HD + 16, CHUNK), BF16),
            pltpu.VMEM((2, HD, WIDE), F32),
            pltpu.VMEM((2, 1, WIDE), F32),
            pltpu.VMEM((2, 1, WIDE), F32),
        ],
        compiler_params=PARAMS,
        cost_estimate=cost(96, 2),
        name="forward",
    )(at, whole, near, far, *kvs)


def backward(shifts, first, last, at, q, lse, kvs, more):
    outs = [shape_of(PART, F32 if s == 0 else BF16) for s in shifts]
    scratch = [pltpu.VMEM(PART, F32)]
    specs = [VMEM] * (2 + len(kvs) + len(more))
    if first:
        outs += [shape_of(ROWS, BF16), shape_of((2, PAIRS, 1, 2 * CHUNK), F32), shape_of(DQT, F32)]
    elif not last:
        outs += [shape_of(DQT, F32)]
    else:
        outs += [shape_of(SIDE, BF16), shape_of(SIDE, BF16)]
        specs[-1] = HBM
        scratch = [pltpu.VMEM(DQT, F32)] + scratch
        scratch += [pltpu.VMEM(DQT, F32), pltpu.SemaphoreType.DMA]
    return pl.pallas_call(
        functools.partial(backward_kernel, shifts, first, last),
        out_shape=tuple(outs),
        in_specs=[SMEM] + specs,
        out_specs=(VMEM,) * len(outs),
        scratch_shapes=scratch,
        compiler_params=PARAMS,
        cost_estimate=cost(24 * len(shifts), 5),
        name="backward" + "".join(map(str, shifts)),
    )(at, q, lse, *kvs, *more)


def project(at, xs, gs):
    x_spec = pl.BlockSpec((4, 256, HALF), lambda i: (0, i, 0))
    g_spec = pl.BlockSpec(PART, lambda i: (0, 0))
    return pl.pallas_call(
        project_kernel,
        grid=(4,),
        out_shape=(shape_of((4, 2, 32, 2 * HD), BF16),) * 4,
        in_specs=[SMEM] + [x_spec] * 4 + [g_spec] * 4,
        out_specs=(pl.BlockSpec((1, 2, 32, 2 * HD), lambda i: (i, 0, 0, 0)),) * 4,
        scratch_shapes=[pltpu.VMEM((256, 2 * HD), F32)],
        compiler_params=PARAMS,
        cost_estimate=pl.CostEstimate(
            flops=2 * 1024 * 2048 * 256, bytes_accessed=6 << 20, transcendentals=0
        ),
        name="project",
    )(at, *[rows.reshape(4, 1024, HALF) for rows in xs], *gs)


def finish(terms):
    return pl.pallas_call(
        finish_kernel,
        out_shape=shape_of((16, 2 * KVH * HD), F32),
        in_specs=[VMEM],
        out_specs=VMEM,
        compiler_params=PARAMS,
        name="finish",
    )(terms)


def cut(at, rows):
    return pl.pallas_call(
        cut_kernel,
        out_shape=shape_of((HALF, 2 * HEADS * HD), BF16),
        in_specs=[SMEM, HBM],
        out_specs=HBM,
        scratch_shapes=[pltpu.SemaphoreType.DMA],
        compiler_params=PARAMS,
        name="cut",
    )(at, rows)


def cut_far(at, rows, near):
    return pl.pallas_call(
        cut_far_kernel,
        out_shape=shape_of(SIDE, BF16),
        in_specs=[SMEM, HBM, HBM],
        out_specs=HBM,
        scratch_shapes=[pltpu.SemaphoreType.DMA((2,))],
        compiler_params=PARAMS,
        name="cut_far",
    )(at, rows, near)


def split_kernel(at, key, value, own, near, far, both):
    z, core = at[1], at[2]
    for dz, dc, out in ((0, 0, own), (0, 1, near), (1, 0, far), (1, 1, both)):
        lo = pl.multiple_of(((core ^ dc) * 2 + (z ^ dz)) * HD, HD)
        out[:, :HD] = key[:, pl.ds(lo, HD)]
        out[:, HD:] = value[:, pl.ds(lo, HD)]


def split_pairs(at, key, value):
    return pl.pallas_call(
        split_kernel,
        out_shape=(shape_of((HALF, 2 * HD), BF16),) * 4,
        in_specs=[SMEM, VMEM, VMEM],
        out_specs=(VMEM,) * 4,
        compiler_params=PARAMS,
        name="split_pairs",
    )(at, key, value)


def half(width, i):
    return pl.BlockSpec((HALF, width), lambda _: (i, 0))


def send_far(*sides):
    rows, width = HALF * len(sides), sides[0].shape[1]
    return pl.pallas_call(
        join_kernel,
        grid=(1,),
        out_shape=shape_of((rows, width), sides[0].dtype),
        in_specs=[half(width, 1)] * len(sides),
        out_specs=pl.BlockSpec((rows, width), lambda _: (0, 0)),
        compiler_params=PARAMS,
        name="send_far",
    )(*sides)


def collect(at, mine, near, far, first=0, paired=False):
    width = mine.shape[1]
    if paired:
        shapes = (shape_of((HALF, KVH * HD), mine.dtype),) * 2
        specs = (pl.BlockSpec((HALF, KVH * HD), lambda _: (0, 0)),) * 2
    else:
        shapes = shape_of((HALF, KVH * width), mine.dtype)
        specs = pl.BlockSpec((HALF, KVH * width), lambda _: (0, 0))
    return pl.pallas_call(
        collect_pairs_kernel if paired else collect_kernel,
        grid=(1,),
        out_shape=shapes,
        in_specs=[SMEM] + [half(width, i) for i in (0, 0, first, first + 1)],
        out_specs=specs,
        compiler_params=PARAMS,
        name="collect",
    )(at, mine, near, far, far)


def join(*parts):
    rows, width = parts[0].shape
    return pl.pallas_call(
        join_kernel,
        out_shape=shape_of((rows * len(parts), width), parts[0].dtype),
        in_specs=[VMEM] * len(parts),
        out_specs=VMEM,
        compiler_params=PARAMS,
        name="join",
    )(*parts)


def turn(at, rows, token):
    return pl.pallas_call(
        turn_kernel,
        out_shape=(shape_of((1024, HALF), rows.dtype),) * 4,
        in_specs=[SMEM, VMEM, HBM],
        out_specs=(VMEM,) * 4,
        compiler_params=PARAMS,
        name="turn",
    )(at, rows, token)


SWAP = [(0, 1), (1, 0)]


def swap(a, axis):
    return lax.ppermute(a, axis, SWAP)


def swap_both(a):
    return lax.ppermute(a, ("zl", "core"), [(0, 3), (1, 2), (2, 1), (3, 0)])


def shift(a, axis, s):
    return lax.ppermute(a, axis, [(i, (i + s) & 3) for i in range(4)])


def tie(*arrays):
    return lax.optimization_barrier(arrays)


def local(query, key, value, d_out, layer_input):
    x, z = lax.axis_index("x"), lax.axis_index("zl")
    y, core = lax.axis_index("y"), lax.axis_index("core")
    at = jnp.stack([y, z, core, x]).astype(jnp.int32)
    query, key, value, d_out = query[0], key[0], value[0], d_out[0]
    layer_input = layer_input[0]

    own, near, far, both = split_pairs(at, key, value)
    far, both, near = swap(far, "zl"), swap_both(both), swap(near, "core")
    near, query = tie(near, query)
    q_near = swap(cut(at, query), "core")
    far, both, near, q_send = tie(far, both, near, cut_far(at, query, q_near))
    kv = join(own, near, far, both)
    kvs = [kv] + [shift(kv, "y", s) for s in (1, 2, 3)]
    q_far = swap(q_send, "zl")
    x_near = turn(at, layer_input, kv)
    x_near = [x_near[0]] + [shift(x_near[s], "x", s) for s in (1, 2, 3)]
    grad_near = swap(cut(at, d_out), "core")
    q_far, grad_send = tie(q_far, cut_far(at, d_out, grad_near))
    grad_far = swap(grad_send, "zl")

    out, out_other, lse, q = forward(at, query, q_near, q_far, kvs)
    lse, *x_near = tie(lse, *x_near)
    x_near = join(*x_near)
    x_far = swap(x_near, "zl")
    part2, grad, row_dot, dq = backward(
        (2,), True, False, at, q, lse, kvs[2:3], (d_out, grad_near, grad_far, out, out_other)
    )
    part3, part1, dq = backward(
        (3, 1), False, False, at, q, lse, kvs[3:0:-2], (grad, row_dot, dq)
    )
    x_near_other, out_near = swap(x_near, "core"), swap(out_other, "core")
    row_dot, x_near_other, out_near, back2 = tie(
        row_dot, x_near_other, out_near, shift(part2, "y", -2)
    )
    own, dq, dq_other = backward(
        (0,), False, True, at, q, lse, kvs[:1], (grad, row_dot, dq)
    )
    back = [shift(part3, "y", -3), back2, shift(part1, "y", -1)]
    joined = own
    for part in back:
        joined = joined + part.astype(F32)
    joined = joined.astype(BF16)
    dq_near = swap(dq_other, "core")
    far = send_far(out, out_near, dq, dq_near)
    joined, x_far, far = tie(joined, x_far, far)
    gs = [joined] + [shift(joined, "x", s) for s in (1, 2, 3)]
    x_far_other = swap(x_far, "core")
    far = swap(far, "zl")
    terms = project(at, (x_near, x_far, x_near_other, x_far_other), gs)

    joined, out, dq, terms0 = tie(joined, out, dq, terms[0])
    total = terms0.astype(F32)
    for i in (1, 2, 3):
        total = total + shift(terms[i], "y", i).astype(F32)
    sides = joined.reshape(2, 2, HALF, 2 * HD)
    mine, other = sides[:, 0].reshape(CHUNK, 2 * HD), sides[:, 1].reshape(CHUNK, 2 * HD)
    near = swap(other, "core")
    sent, far = tie(send_far(mine, near), far)
    d_key, d_value = collect(at, mine, near, swap(sent, "zl"), paired=True)
    attn_out = collect(at, out, out_near, far)
    d_query = collect(at, dq, dq_near, far, first=2)

    total, attn_out, d_query, d_key, d_value = tie(
        total.astype(BF16), attn_out, d_query, d_key, d_value
    )
    terms = lax.all_to_all(
        total.reshape(16, 16, 2 * HD), ("zh", "zl", "core"), split_axis=0, concat_axis=0, tiled=True
    )
    return attn_out[None], d_query[None], d_key[None], d_value[None], finish(terms)


def solution(mesh):
    parts = jax.sharding.Mesh(mesh.devices.reshape(4, 4, 2, 4, 2), ("x", "zh", "zl", "y", "core"))
    tokens = P(("x", "zh"), ("zl", "y", "core"), None)
    return jax.shard_map(
        local,
        mesh=parts,
        in_specs=(tokens,) * 5,
        out_specs=(tokens,) * 4 + (P(("x", "zh", "zl", "y", "core"), None),),
        check_vma=False,
    )
```
